256 devices in a mesh: dp: 8 (over y, z_lo), expert: 32 (over z_hi, x, core).
Axes of the slice: x: 4, y: 4, z: 8 (z_hi: 4, z_lo: 2; z = z_hi * 2 + z_lo), core: 2. Of those that a mesh axis runs over, the one named last changes fastest.
Arguments:
- tokens: bfloat16 [65536, 1024], P(('dp', 'expert')), may hold values from -6 to 6
- cotangent: bfloat16 [65536, 1024], P(('dp', 'expert')), may hold values from -1.1953125 to 1.1953125
- prob: bfloat16 [65536], P(('dp', 'expert')), may hold values from 0.19921875 to 1
- assign: int32 [65536, 1], P(('dp', 'expert')), may hold values from 0 to 31; in each aligned block of 256 rows (0 to 255, 256 to 511, ...) at most 24 rows name the same one
- w_gate: bfloat16 [32, 1024, 1024], P('expert'), may hold values from -0.1875 to 0.1875
- w_up: bfloat16 [32, 1024, 1024], P('expert'), may hold values from -0.1875 to 0.1875
- w_down: bfloat16 [32, 1024, 1024], P('expert'), may hold values from -0.1875 to 0.1875
Outputs:
- grad_tokens: bfloat16 [65536, 1024], P(('dp', 'expert'))
- grad_prob: bfloat16 [65536], P(('dp', 'expert'))
- grad_gate: float32 [32, 1024, 1024], P('expert', 'dp')
- grad_up: float32 [32, 1024, 1024], P('expert', 'dp')
- grad_down: float32 [32, 1024, 1024], P('expert', 'dp')
The draws below stay inside these ranges and needn't reach their ends.
Inputs may be any that keep to these rules, and one draw needn't show every extreme that they name: `assign`: among the 256 tokens of one device (aligned blocks of rows), at most 24 are assigned to one expert, and in every draw some expert receives exactly 24 tokens of some device.
All inputs are finite; a program needn't handle non-finite values.
Results may differ from the reference program's by a relative error of at most 0.015.
Values may be sent and summed in bfloat16 or wider, within the bound.
No kernel may reach another device: no remote copies, remote signals or barrier semaphores. Data moves between devices by JAX's collectives and lax.ppermute only.
A program may use at most 128 MiB of HBM per device.

```python
import math
import jax
import jax.numpy as jnp
import numpy as np
from jax import lax

D = 1024
FF = 1024
TOK_DEV = 256
EXPERTS = 32
GROUPS = 8
MOST = 24
TOKENS = 65536


def block_scale(rng, dims, cuts, smallest, top_value):
    def one(dim, parts):
        heights = jax.random.uniform(jax.random.fold_in(jax.random.fold_in(rng, 6), dim), (parts,), jnp.float32, smallest / len(cuts), top_value / len(cuts))
        return jnp.repeat(jnp.exp(heights), dims[dim] // parts).reshape((-1,) + (1,) * (len(dims) - dim - 1))

    level = one(*cuts[0])
    for cut in cuts[1:]:
        level = level * one(*cut)
    return level


def assign_block(stream_key, own, number, rows, number_of, top, limit, skew):
    sequence = jax.random.permutation(stream_key, number_of)
    heavy_load, ordinary = portions_of(number_of, rows * top, limit, skew, True), portions_of(number_of, rows * top, limit, skew, False)
    places = jnp.arange(number_of)

    def named(sizes, turn):
        used = int((sizes > 0).sum())
        fixed = max(1, used // 4)
        passed = fixed + (places - fixed + turn * (used - fixed)) % max(1, number_of - fixed)
        return jnp.zeros((number_of,), jnp.int32).at[sequence[jnp.where(places < fixed, places, passed)]].set(jnp.asarray(sizes, jnp.int32))

    sizes = jnp.where(number % 4 == 0, named(heavy_load, number // 4), named(ordinary, number - number // 4 - 1))
    mixed = jax.random.permutation(jax.random.fold_in(own, 3), number_of)
    giver, sink = mixed[0:number_of // 2 * 2:2], mixed[1:number_of // 2 * 2:2]
    room = jnp.minimum(sizes[giver] - 1, limit - sizes[sink]) // 2
    room = jnp.where((giver == sequence[0]) | (sink == sequence[0]) | (sizes[sink] == 0), 0, jnp.maximum(room, 0))
    passed = jax.random.randint(jax.random.fold_in(own, 4), (number_of // 2,), 0, 1 << 20) % (room + 1)
    sizes = sizes.at[giver].add(-passed).at[sink].add(passed)
    labels = jnp.searchsorted(jnp.cumsum(sizes), jnp.arange(rows * top), side="right").astype(jnp.int32)
    grid = labels.reshape(top, rows).T
    grid = grid[jax.random.permutation(jax.random.fold_in(own, 1), rows)]
    turn = jax.random.randint(jax.random.fold_in(own, 2), (rows, 1), 0, top)
    return jnp.take_along_axis(grid, (jnp.arange(top)[None, :] + turn) % top, axis=1)


def portions_of(number_of, total, limit, slope, full):
    loads = [(1 << 20) // math.isqrt(rank ** slope) + 1 for rank in range(1, number_of + 1)]
    largest = limit if full else min(limit, max(-(-total // number_of), total * loads[0] // sum(loads)))
    least = 1 if total - largest >= number_of - 1 else 0
    given, spare = [largest] + [least] * (number_of - 1), total - largest - least * (number_of - 1)
    while spare > 0:
        candidates = [i for i in range(1, number_of) if given[i] < largest] or [i for i in range(1, number_of) if given[i] < limit]
        mass, remaining = sum([loads[i] for i in candidates]), spare
        for i in candidates:
            extra = min(limit - given[i], max(1, remaining * loads[i] // mass), spare)
            given[i] = given[i] + extra
            spare = spare - extra
    return np.array(given)


def bell_draw(own_key, extent, spread, bound, split=(), held_as=jnp.bfloat16):
    values = spread * jax.random.normal(own_key, extent, jnp.float32)
    if split:
        values = values * block_scale(own_key, extent, split, -0.22, 0.18)
    return jnp.clip(values, -bound, bound).astype(held_as)


def setup_inputs(seed: int = 0) -> dict:
    streams_of = jax.random.split(jax.random.key(seed), 8)
    tokens = bell_draw(streams_of[0], (TOKENS, D), 1.0, 6.0, ((0, 256),))
    cotangent = bell_draw(streams_of[1], (TOKENS, D), 0.2, 1.1953125, ((0, 256),))
    prob = jnp.clip(0.19921875 + 0.80078125 * jax.random.uniform(streams_of[2], (TOKENS,), jnp.float32) ** block_scale(streams_of[2], (TOKENS,), ((0, 256),), -0.2, 0.2), 0.19921875, 1.0).astype(jnp.bfloat16)
    assign_keys = jax.random.split(jax.random.fold_in(streams_of[3], 1), TOKENS // TOK_DEV)
    assign_turns = jax.random.permutation(jax.random.fold_in(streams_of[3], 3), TOKENS // TOK_DEV)
    assign = jax.vmap(lambda own, number: assign_block(jax.random.fold_in(streams_of[3], 2), own, number, TOK_DEV, EXPERTS, 1, MOST, 2))(assign_keys, assign_turns).reshape((TOKENS, 1))
    w_gate = bell_draw(streams_of[4], (EXPERTS, D, FF), D ** -0.5, 0.1875, ((0, 32),))
    w_up = bell_draw(streams_of[5], (EXPERTS, D, FF), D ** -0.5, 0.1875, ((0, 32),))
    w_down = bell_draw(streams_of[6], (EXPERTS, FF, D), FF ** -0.5, 0.1875, ((0, 32),))
    return {"tokens": tokens, "cotangent": cotangent, "prob": prob, "assign": assign, "w_gate": w_gate, "w_up": w_up, "w_down": w_down}


def placement_of(assign_dev):
    chosen = (assign_dev[:, None] == jnp.arange(EXPERTS, dtype=jnp.int32)[None, :]).astype(jnp.int32)
    before = jnp.cumsum(chosen, axis=0) - chosen
    position = jnp.sum(before * chosen, axis=1).astype(jnp.int32)
    slot = assign_dev * MOST + position
    return jnp.arange(EXPERTS * MOST, dtype=jnp.int32)[:, None] == slot[None, :]


def expert_pass(rows_in, cot_in, prob_in, gate_weight, up_weight, down_weight):
    gate = jnp.dot(rows_in, gate_weight, preferred_element_type=jnp.float32)
    up = jnp.dot(rows_in, up_weight, preferred_element_type=jnp.float32)
    sigmoid_gate = jax.nn.sigmoid(gate)
    activation = gate * sigmoid_gate
    hidden = (activation * up).astype(jnp.bfloat16)
    expert_out = jnp.dot(hidden, down_weight, preferred_element_type=jnp.float32)
    grad_prob = jnp.sum(cot_in.astype(jnp.float32) * expert_out, axis=1).astype(jnp.bfloat16)
    scaled = (prob_in.astype(jnp.float32)[:, None] * cot_in.astype(jnp.float32)).astype(jnp.bfloat16)
    grad_hidden = lax.dot_general(scaled, down_weight, (((1,), (1,)), ((), ())), preferred_element_type=jnp.float32)
    grad_gate_pre = (grad_hidden * up * sigmoid_gate * (1.0 + gate * (1.0 - sigmoid_gate))).astype(jnp.bfloat16)
    grad_up_pre = (grad_hidden * activation).astype(jnp.bfloat16)
    grad_rows = lax.dot_general(grad_gate_pre, gate_weight, (((1,), (1,)), ((), ())), preferred_element_type=jnp.float32)
    grad_rows = grad_rows + lax.dot_general(grad_up_pre, up_weight, (((1,), (1,)), ((), ())), preferred_element_type=jnp.float32)
    grad_rows = grad_rows.astype(jnp.bfloat16)
    part_gate = lax.dot_general(rows_in, grad_gate_pre, (((0,), (0,)), ((), ())), preferred_element_type=jnp.float32)
    part_up = lax.dot_general(rows_in, grad_up_pre, (((0,), (0,)), ((), ())), preferred_element_type=jnp.float32)
    part_down = lax.dot_general(hidden, scaled, (((0,), (0,)), ((), ())), preferred_element_type=jnp.float32)
    return grad_rows, grad_prob, part_gate, part_up, part_down


def rounded(value):
    return lax.optimization_barrier(value.astype(jnp.bfloat16)).astype(jnp.float32)


def reference(tokens, cotangent, prob, assign, w_gate, w_up, w_down):
    devices = GROUPS * EXPERTS
    slots_all = EXPERTS * MOST
    tok_split = tokens.reshape(devices, TOK_DEV, D)
    cot_split = cotangent.reshape(devices, TOK_DEV, D)
    prob_split = prob.reshape(devices, TOK_DEV)
    assign_split = assign.reshape(devices, TOK_DEV).astype(jnp.int32)

    def gather_slots(item):
        tok_dev, cot_dev, prob_dev, assign_dev = item
        place = placement_of(assign_dev)
        weights = place.astype(jnp.bfloat16)
        send_rows = jnp.dot(weights, tok_dev, preferred_element_type=jnp.float32).astype(jnp.bfloat16)
        send_cot = jnp.dot(weights, cot_dev, preferred_element_type=jnp.float32).astype(jnp.bfloat16)
        send_prob = jnp.sum(jnp.where(place, prob_dev[None, :].astype(jnp.float32), 0.0), axis=1).astype(jnp.bfloat16)
        return send_rows, send_cot, send_prob

    send_rows, send_cot, send_prob = lax.map(gather_slots, (tok_split, cot_split, prob_split, assign_split))
    rows_by_expert = send_rows.reshape(GROUPS, EXPERTS, EXPERTS, MOST, D).transpose(2, 0, 1, 3, 4).reshape(EXPERTS, GROUPS, slots_all, D)
    cot_by_expert = send_cot.reshape(GROUPS, EXPERTS, EXPERTS, MOST, D).transpose(2, 0, 1, 3, 4).reshape(EXPERTS, GROUPS, slots_all, D)
    prob_by_expert = send_prob.reshape(GROUPS, EXPERTS, EXPERTS, MOST).transpose(2, 0, 1, 3).reshape(EXPERTS, GROUPS, slots_all)

    def per_expert(item):
        rows_e, cot_e, prob_e, gate_weight, up_weight, down_weight = item

        def per_group(carry, inner):
            rows_in, cot_in, prob_in = inner
            grad_rows, grad_pr, part_gate, part_up, part_down = expert_pass(rows_in, cot_in, prob_in, gate_weight, up_weight, down_weight)
            carry = (carry[0] + rounded(part_gate), carry[1] + rounded(part_up), carry[2] + rounded(part_down))
            return carry, (grad_rows, grad_pr)

        start = (jnp.zeros((D, FF), jnp.float32), jnp.zeros((D, FF), jnp.float32), jnp.zeros((FF, D), jnp.float32))
        carry, (grad_rows, grad_pr) = lax.scan(per_group, start, (rows_e, cot_e, prob_e))
        return grad_rows, grad_pr, carry[0], carry[1], carry[2]

    grad_rows, grad_pr, grad_gate, grad_up, grad_down = lax.map(per_expert, (rows_by_expert, cot_by_expert, prob_by_expert, w_gate, w_up, w_down))
    back_rows = grad_rows.reshape(EXPERTS, GROUPS, EXPERTS, MOST, D).transpose(1, 2, 0, 3, 4).reshape(devices, slots_all, D)
    back_prob = grad_pr.reshape(EXPERTS, GROUPS, EXPERTS, MOST).transpose(1, 2, 0, 3).reshape(devices, slots_all)

    def scatter_back(item):
        rows_back, prob_back, assign_dev = item
        place = placement_of(assign_dev)
        weights = place.astype(jnp.bfloat16)
        grad_tok = lax.dot_general(weights, rows_back, (((0,), (0,)), ((), ())), preferred_element_type=jnp.float32).astype(jnp.bfloat16)
        grad_p = jnp.sum(jnp.where(place, prob_back[:, None].astype(jnp.float32), 0.0), axis=0).astype(jnp.bfloat16)
        return grad_tok, grad_p

    grad_tokens, grad_prob = lax.map(scatter_back, (back_rows, back_prob, assign_split))
    return grad_tokens.reshape(TOKENS, D), grad_prob.reshape(TOKENS), grad_gate, grad_up, grad_down
```

```python
import jax
import jax.numpy as jnp
from jax import lax
from jax.sharding import PartitionSpec as P


def placement_of(assign_dev, experts, capacity):
    chosen = (assign_dev[:, None] == jnp.arange(experts, dtype=jnp.int32)[None, :]).astype(
        jnp.int32
    )
    before = jnp.cumsum(chosen, axis=0) - chosen
    position = jnp.sum(before * chosen, axis=1)
    slot = assign_dev * capacity + position
    return jnp.arange(experts * capacity, dtype=jnp.int32)[:, None] == slot[None, :]


def recompute(rows_in, gate_weight, up_weight, down_weight):
    gate = jnp.dot(rows_in, gate_weight, preferred_element_type=jnp.float32)
    up = jnp.dot(rows_in, up_weight, preferred_element_type=jnp.float32)
    sigmoid_gate = jax.nn.sigmoid(gate)
    activation = gate * sigmoid_gate
    hidden = (activation * up).astype(jnp.bfloat16)
    expert_out = jnp.dot(hidden, down_weight, preferred_element_type=jnp.float32)
    return (gate, up, sigmoid_gate, activation, hidden, expert_out)


AXES = ("dp", "expert")


def shift_y(value, step):
    pairs = []
    for dp in range(8):
        y, low = divmod(dp, 2)
        pairs.append((dp, ((y + step) % 4) * 2 + low))
    return lax.ppermute(value, "dp", pairs)


def swap_low(value):
    return lax.ppermute(value, "dp", [(dp, dp ^ 1) for dp in range(8)])


def summed_parts(pairs):
    index = lax.axis_index("dp")
    y, low = index // 2, index % 2
    half = 512

    def chunk(pair, offset):
        left, right = pair
        start = ((y + offset) % 4) * 256
        piece = lax.dynamic_slice_in_dim(left, start, 256, axis=1)
        return lax.dot_general(
            piece, right, (((0,), (0,)), ((), ())), preferred_element_type=jnp.float32
        )

    far = [chunk(pair, 2).astype(jnp.bfloat16) for pair in pairs]
    first = [(shift_y(f[:, :half], 1), shift_y(f[:, half:], -1)) for f in far]
    second = []
    for pair, (from_left, from_right) in zip(pairs, first):
        up_part = chunk(pair, 1)
        down_part = chunk(pair, 3)
        up_part = jnp.concatenate(
            [up_part[:, :half] + from_left.astype(jnp.float32), up_part[:, half:]], axis=1
        ).astype(jnp.bfloat16)
        down_part = jnp.concatenate(
            [down_part[:, :half], down_part[:, half:] + from_right.astype(jnp.float32)], axis=1
        ).astype(jnp.bfloat16)
        second.append((shift_y(up_part, 1), shift_y(down_part, -1)))
    own = [chunk(pair, 0) for pair in pairs]
    results = []
    for mine, (from_left, from_right) in zip(own, second):
        total = mine + from_left.astype(jnp.float32) + from_right.astype(jnp.float32)
        away = lax.dynamic_slice_in_dim(total, (1 - low) * 128, 128, axis=0)
        keep = lax.dynamic_slice_in_dim(total, low * 128, 128, axis=0)
        other = swap_low(away.astype(jnp.bfloat16))
        results.append((keep + other.astype(jnp.float32))[None])
    return results


def local(tokens, cotangent, prob, assign, w_gate, w_up, w_down):
    experts = lax.axis_size("expert")
    tok_rows = tokens.shape[0]
    width = tokens.shape[1]
    capacity = 3 * tok_rows // experts
    slots_all = experts * capacity
    gate_weight = w_gate[0]
    up_weight = w_up[0]
    down_weight = w_down[0]
    place = placement_of(assign[:, 0], experts, capacity)
    weights = place.astype(jnp.bfloat16)
    send_rows = (
        jnp.dot(weights, tokens, preferred_element_type=jnp.float32)
        .astype(jnp.bfloat16)
        .reshape(experts, capacity, width)
    )
    send_cot = (
        jnp.dot(weights, cotangent, preferred_element_type=jnp.float32)
        .astype(jnp.bfloat16)
        .reshape(experts, capacity, width)
    )
    send_prob = (
        jnp.sum(jnp.where(place, prob[None, :].astype(jnp.float32), 0.0), axis=1)
        .astype(jnp.bfloat16)
        .reshape(experts, capacity)
    )
    recv_rows, recv_cot, recv_prob = (
        lax.all_to_all(send_rows, "expert", split_axis=0, concat_axis=0, tiled=True),
        lax.all_to_all(send_cot, "expert", split_axis=0, concat_axis=0, tiled=True),
        lax.all_to_all(send_prob, "expert", split_axis=0, concat_axis=0, tiled=True),
    )
    rows_in = recv_rows.reshape(slots_all, width)
    gate, up, sigmoid_gate, activation, hidden, expert_out = recompute(
        rows_in, gate_weight, up_weight, down_weight
    )
    cot_in = recv_cot.reshape(slots_all, width)
    prob_in = recv_prob.reshape(slots_all)
    grad_pr = jnp.sum(cot_in.astype(jnp.float32) * expert_out, axis=1).astype(jnp.bfloat16)
    scaled = (prob_in.astype(jnp.float32)[:, None] * cot_in.astype(jnp.float32)).astype(
        jnp.bfloat16
    )
    grad_hidden = lax.dot_general(
        scaled, down_weight, (((1,), (1,)), ((), ())), preferred_element_type=jnp.float32
    )
    grad_gate_pre = (grad_hidden * up * sigmoid_gate * (1.0 + gate * (1.0 - sigmoid_gate))).astype(
        jnp.bfloat16
    )
    grad_up_pre = (grad_hidden * activation).astype(jnp.bfloat16)
    grad_rows = lax.dot_general(
        grad_gate_pre, gate_weight, (((1,), (1,)), ((), ())), preferred_element_type=jnp.float32
    )
    grad_rows = grad_rows + lax.dot_general(
        grad_up_pre, up_weight, (((1,), (1,)), ((), ())), preferred_element_type=jnp.float32
    )
    grad_rows = grad_rows.astype(jnp.bfloat16)
    back_rows, back_prob = (
        lax.all_to_all(
            grad_rows.reshape(experts, capacity, width),
            "expert",
            split_axis=0,
            concat_axis=0,
            tiled=True,
        ),
        lax.all_to_all(
            grad_pr.reshape(experts, capacity), "expert", split_axis=0, concat_axis=0, tiled=True
        ),
    )
    grad_tokens = lax.dot_general(
        weights,
        back_rows.reshape(slots_all, width),
        (((0,), (0,)), ((), ())),
        preferred_element_type=jnp.float32,
    ).astype(jnp.bfloat16)
    grad_prob = jnp.sum(
        jnp.where(place, back_prob.reshape(slots_all)[:, None].astype(jnp.float32), 0.0), axis=0
    ).astype(jnp.bfloat16)
    grad_down, grad_gate, grad_up = summed_parts(
        ((hidden, scaled), (rows_in, grad_gate_pre), (rows_in, grad_up_pre))
    )
    return (grad_tokens, grad_prob, grad_gate, grad_up, grad_down)


def solution(mesh):
    placed = (
        P(("dp", "expert"), None),
        P(("dp", "expert"), None),
        P(("dp", "expert")),
        P(("dp", "expert"), None),
        P("expert", None, None),
        P("expert", None, None),
        P("expert", None, None),
    )
    return jax.shard_map(
        local,
        mesh=mesh,
        in_specs=placed,
        out_specs=(
            P(("dp", "expert"), None),
            P(("dp", "expert")),
            P("expert", "dp", None),
            P("expert", "dp", None),
            P("expert", "dp", None),
        ),
        check_vma=False,
    )
```

```python
import jax
import jax.numpy as jnp
from jax import lax
from jax.sharding import PartitionSpec as P


def shift_y(value, step):
    pairs = []
    for dp in range(8):
        y, low = divmod(dp, 2)
        pairs.append((dp, ((y + step) % 4) * 2 + low))
    return lax.ppermute(value, "dp", pairs)


def swap_low(value):
    return lax.ppermute(value, "dp", [(dp, dp ^ 1) for dp in range(8)])


def chunk(pair, y, offset):
    left, right = pair
    start = ((y + offset) % 4) * 256
    piece = lax.dynamic_slice_in_dim(left, start, 256, axis=1)
    return lax.dot_general(
        piece, right, (((0,), (0,)), ((), ())), preferred_element_type=jnp.float32
    )


HALF = 512


def far_part(pair):
    return chunk(pair, lax.axis_index("dp") // 2, 2).astype(jnp.bfloat16)


def first_step(far):
    return shift_y(far[:, :HALF], 1), shift_y(far[:, HALF:], -1)


def second_values(pair, got):
    y = lax.axis_index("dp") // 2
    from_left, from_right = got
    up_part = chunk(pair, y, 1)
    down_part = chunk(pair, y, 3)
    up_part = jnp.concatenate(
        [up_part[:, :HALF] + from_left.astype(jnp.float32), up_part[:, HALF:]], axis=1
    )
    down_part = jnp.concatenate(
        [down_part[:, :HALF], down_part[:, HALF:] + from_right.astype(jnp.float32)], axis=1
    )
    return up_part.astype(jnp.bfloat16), down_part.astype(jnp.bfloat16)


def second_step(values):
    return shift_y(values[0], 1), shift_y(values[1], -1)


def third_values(pair, got):
    index = lax.axis_index("dp")
    low = index % 2
    total = chunk(pair, index // 2, 0) + got[0].astype(jnp.float32) + got[1].astype(jnp.float32)
    away = lax.dynamic_slice_in_dim(total, (1 - low) * 128, 128, axis=0)
    keep = lax.dynamic_slice_in_dim(total, low * 128, 128, axis=0)
    return keep, away.astype(jnp.bfloat16)


def third_step(values):
    return (values[0] + swap_low(values[1]).astype(jnp.float32))[None]


def summed_part(pair):
    got = first_step(far_part(pair))
    got = second_step(second_values(pair, got))
    return third_step(third_values(pair, got))


def after(values, *others):
    return lax.optimization_barrier((values, others))[0]


def turned(a, b):
    return lax.dot_general(a, b, (((1,), (1,)), ((), ())), preferred_element_type=jnp.float32)


def gated(rows_in, gate_weight, up_weight):
    gate = jnp.dot(rows_in, gate_weight, preferred_element_type=jnp.float32)
    up = jnp.dot(rows_in, up_weight, preferred_element_type=jnp.float32)
    return gate, up


def factors(gate, up):
    sigmoid_gate = jax.nn.sigmoid(gate)
    activation = gate * sigmoid_gate
    hidden = (activation * up).astype(jnp.bfloat16)
    slope = up * sigmoid_gate * (1.0 + gate * (1.0 - sigmoid_gate))
    return hidden, activation, slope


def expert_back(grad_hidden, hidden, activation, slope):
    grad_gate_pre = (grad_hidden * slope).astype(jnp.bfloat16)
    grad_up_pre = (grad_hidden * activation).astype(jnp.bfloat16)
    moved = jnp.sum(hidden.astype(jnp.float32) * grad_hidden, axis=1)
    return grad_gate_pre, grad_up_pre, moved


CAPACITY = 24
NOTES = 128


def exchange(value):
    devices = lax.axis_size("expert")
    blocks = value.reshape(devices, CAPACITY, value.shape[1])
    blocks = lax.all_to_all(blocks, "expert", split_axis=0, concat_axis=0, tiled=True)
    return blocks.reshape(value.shape)


def local(tokens, cotangent, prob, assign, w_gate, w_up, w_down):
    gate_weight, up_weight, down_weight = w_gate[0], w_up[0], w_down[0]
    count, width = tokens.shape
    slots = lax.axis_size("expert") * CAPACITY
    named = assign[:, 0]
    order = jnp.arange(count, dtype=jnp.int32)
    same = (order[:, None] < order[None, :]) & (assign == named[None, :])
    slot = named * CAPACITY + jnp.sum(same.astype(jnp.int32), axis=0)
    pick = (jnp.arange(slots, dtype=jnp.int32)[:, None] == slot[None, :]).astype(jnp.bfloat16)
    scaled = (prob.astype(jnp.float32)[:, None] * cotangent.astype(jnp.float32)).astype(
        jnp.bfloat16
    )

    def gather(value):
        return jnp.dot(pick, value, preferred_element_type=jnp.float32).astype(jnp.bfloat16)

    rows_in = exchange(gather(tokens))
    scaled_in = exchange(after(gather(scaled), rows_in))
    hidden, activation, slope = lax.optimization_barrier(
        factors(*gated(rows_in, gate_weight, up_weight))
    )
    far_down = far_part((hidden, scaled_in))
    first_down = first_step(far_down)
    grad_hidden = turned(scaled_in, down_weight)
    grad_gate_pre, grad_up_pre, moved = expert_back(grad_hidden, hidden, activation, slope)
    far_gate = far_part((rows_in, grad_gate_pre))
    far_up = far_part((rows_in, grad_up_pre))
    first_gate = first_step(far_gate)
    first_up = first_step(far_up)
    grad_gate_pre, grad_up_pre = after((grad_gate_pre, grad_up_pre), far_gate, far_up)
    grad_rows = (turned(grad_gate_pre, gate_weight) + turned(grad_up_pre, up_weight)).astype(
        jnp.bfloat16
    )
    notes = jnp.broadcast_to(moved.astype(jnp.bfloat16)[:, None], (slots, NOTES))
    leaving = after(jnp.concatenate([grad_rows, notes], axis=1), first_down)
    home = exchange(leaving)
    pairs = ((hidden, scaled_in), (rows_in, grad_gate_pre), (rows_in, grad_up_pre))
    pairs = after(pairs, leaving)
    parts = []
    for pair, first in zip(pairs, (first_down, first_gate, first_up)):
        second = second_step(second_values(pair, first))
        parts.append(third_step(third_values(pair, second)))
    returned = lax.dot_general(
        pick, home, (((0,), (0,)), ((), ())), preferred_element_type=jnp.float32
    )
    grad_tokens = returned[:, :width].astype(jnp.bfloat16)
    grad_prob = (returned[:, width] / prob.astype(jnp.float32)).astype(jnp.bfloat16)
    return (grad_tokens, grad_prob, parts[1], parts[2], parts[0])


def solution(mesh):
    placed = (
        P(("dp", "expert"), None),
        P(("dp", "expert"), None),
        P(("dp", "expert")),
        P(("dp", "expert"), None),
        P("expert", None, None),
        P("expert", None, None),
        P("expert", None, None),
    )
    return jax.shard_map(
        local,
        mesh=mesh,
        in_specs=placed,
        out_specs=(
            P(("dp", "expert"), None),
            P(("dp", "expert")),
            P("expert", "dp", None),
            P("expert", "dp", None),
            P("expert", "dp", None),
        ),
        check_vma=False,
    )
```

```python
import jax
import jax.numpy as jnp
from jax import lax
from jax.experimental import pallas as pl
from jax.experimental.pallas import tpu as pltpu
from jax.sharding import PartitionSpec as P


def shift_y(value, step):
    pairs = []
    for dp in range(8):
        y, low = divmod(dp, 2)
        pairs.append((dp, ((y + step) % 4) * 2 + low))
    return lax.ppermute(value, "dp", pairs)


def swap_low(value):
    return lax.ppermute(value, "dp", [(dp, dp ^ 1) for dp in range(8)])


HALF = 512
BLOCK = 256
LEFT_TURNED = (((0,), (0,)), ((), ()))
RIGHT_TURNED = (((1,), (1,)), ((), ()))


def product(left, right, dimensions):
    return lax.dot_general(left, right, dimensions, preferred_element_type=jnp.float32)


def call(kernel, outputs, position, inputs, flops):
    in_vmem = pl.BlockSpec(memory_space=pltpu.VMEM)
    in_smem = pl.BlockSpec(memory_space=pltpu.SMEM)
    moved = sum(v.size * v.dtype.itemsize for v in inputs)
    return pl.pallas_call(
        kernel,
        out_shape=outputs,
        in_specs=[in_smem] + [in_vmem] * len(inputs),
        out_specs=[in_vmem] * len(outputs),
        compiler_params=pltpu.CompilerParams(vmem_limit_bytes=16 * 1024 * 1024),
        cost_estimate=pl.CostEstimate(flops=flops, bytes_accessed=moved, transcendentals=0),
    )(position, *inputs)


def columns_of(ref, y, offset):
    start = pl.multiple_of(((y + offset) % 4) * BLOCK, BLOCK)
    return ref[:, pl.ds(start, BLOCK)]


def expert_kernel(
    position,
    both,
    w_gate,
    w_up,
    w_down,
    leaving,
    far_low,
    far_high,
    ready_up,
    ready_down,
    add_up,
    add_down,
    own,
    hidden,
    gate_pre,
    up_pre,
):
    y = position[0]
    width = w_gate.shape[0]
    moved = jnp.zeros((both.shape[0], 1), jnp.float32)
    for start in range(0, w_gate.shape[1], BLOCK):
        cut = pl.ds(start, BLOCK)
        gate = jnp.dot(both[:, :width], w_gate[:, cut], preferred_element_type=jnp.float32)
        up = jnp.dot(both[:, :width], w_up[:, cut], preferred_element_type=jnp.float32)
        grad_hidden = product(both[:, width:], w_down[cut, :], RIGHT_TURNED)
        sigmoid_gate = jax.nn.sigmoid(gate)
        active = gate * sigmoid_gate
        held = (active * up).astype(jnp.bfloat16)
        hidden[:, cut] = held
        slope = sigmoid_gate * (1.0 + gate * (1.0 - sigmoid_gate))
        gate_pre[:, cut] = (grad_hidden * up * slope).astype(jnp.bfloat16)
        up_pre[:, cut] = (grad_hidden * active).astype(jnp.bfloat16)
        part = held.astype(jnp.float32) * grad_hidden
        moved = moved + jnp.sum(part, axis=1, keepdims=True)

    scaled = both.at[:, width:]
    pairs = ((hidden, scaled), (both, gate_pre), (both, up_pre))
    cuts = [pl.ds(place * BLOCK, BLOCK) for place in range(3)]
    for cut, (left, right) in zip(cuts, pairs):
        far = product(columns_of(left, y, 2), right[...], LEFT_TURNED).astype(jnp.bfloat16)
        far_low[cut, :] = far[:, :HALF]
        far_high[cut, :] = far[:, HALF:]
    leaving[:, width:] = jnp.broadcast_to(moved, (both.shape[0], NOTES)).astype(jnp.bfloat16)
    for start in range(0, width, BLOCK):
        cut = pl.ds(start, BLOCK)
        grad = product(gate_pre[...], w_gate[cut, :], RIGHT_TURNED)
        grad = grad + product(up_pre[...], w_up[cut, :], RIGHT_TURNED)
        leaving[:, cut] = grad.astype(jnp.bfloat16)
    for cut, (left, right) in zip(cuts, pairs):
        own[cut, :] = product(columns_of(left, y, 0), right[...], LEFT_TURNED)
    for cut, (left, right) in zip(cuts, pairs):
        part = product(columns_of(left, y, 1), right[...], LEFT_TURNED)
        add_up[cut, :] = part[:, :HALF]
        ready_up[cut, :] = part[:, HALF:].astype(jnp.bfloat16)
        part = product(columns_of(left, y, 3), right[...], LEFT_TURNED)
        add_down[cut, :] = part[:, HALF:]
        ready_down[cut, :] = part[:, :HALF].astype(jnp.bfloat16)


def expert(position, both, w_gate, w_up, w_down):
    slots, width = both.shape[0], w_gate.shape[0]
    size = w_gate.shape[1]
    shapes = [((slots, width + NOTES), jnp.bfloat16)]
    shapes += [((3 * BLOCK, HALF), jnp.bfloat16)] * 4
    shapes += [((3 * BLOCK, HALF), jnp.float32)] * 2
    shapes += [((3 * BLOCK, width), jnp.float32)]
    in_vmem = pl.BlockSpec(memory_space=pltpu.VMEM)
    return pl.pallas_call(
        expert_kernel,
        out_shape=[jax.ShapeDtypeStruct(*shape) for shape in shapes],
        in_specs=[pl.BlockSpec(memory_space=pltpu.SMEM)] + [in_vmem] * 4,
        out_specs=[in_vmem] * len(shapes),
        scratch_shapes=[pltpu.VMEM((slots, size), jnp.bfloat16)] * 3,
        compiler_params=pltpu.CompilerParams(vmem_limit_bytes=24 * 1024 * 1024),
        cost_estimate=pl.CostEstimate(
            flops=16 * slots * width * size, bytes_accessed=20_000_000, transcendentals=0
        ),
    )(position, both, w_gate, w_up, w_down)


def pick_of(slot, slots):
    return (lax.broadcasted_iota(jnp.int32, (slots, slot.shape[1]), 0) == slot).astype(
        jnp.bfloat16
    )


def send_kernel(position, named, prob, tokens, cotangent, both, slot):
    count, width = tokens.shape
    square = (count, count)
    across = jnp.broadcast_to(named[...], square)
    earlier = lax.broadcasted_iota(jnp.int32, square, 0) < lax.broadcasted_iota(
        jnp.int32, square, 1
    )
    same = jnp.where(earlier & (across.T == across), 1, 0)
    slot[...] = named[...] * CAPACITY + jnp.sum(same, axis=0, keepdims=True)
    pick = pick_of(slot[...], both.shape[0])
    both[:, :width] = jnp.dot(pick, tokens[...], preferred_element_type=jnp.float32).astype(
        jnp.bfloat16
    )
    weight = jnp.broadcast_to(prob[...], square).T[:, :1]
    scaled = (weight * cotangent[...].astype(jnp.float32)).astype(jnp.bfloat16)
    both[:, width:] = jnp.dot(pick, scaled, preferred_element_type=jnp.float32).astype(
        jnp.bfloat16
    )


def home_kernel(position, slot, prob, home, grad_tokens, grad_prob):
    width = grad_tokens.shape[1]
    pick = pick_of(slot[...], home.shape[0])
    grad_tokens[...] = product(pick, home[:, :width], LEFT_TURNED).astype(jnp.bfloat16)
    moved = product(home[:, width:], pick, LEFT_TURNED)
    grad_prob[...] = moved[:1, :] / prob[...]


def first_step(low, high):
    return shift_y(low, 1), shift_y(high, -1)


def second_values(up_part, down_part, got):
    up_part = (up_part + got[0].astype(jnp.float32)).astype(jnp.bfloat16)
    down_part = (down_part + got[1].astype(jnp.float32)).astype(jnp.bfloat16)
    return lax.optimization_barrier((up_part, down_part))


def third_step(own, ready, added, low):
    left = jnp.concatenate([added[0], ready[0]], axis=1)
    right = jnp.concatenate([ready[1], added[1]], axis=1)
    total = own + left.astype(jnp.float32) + right.astype(jnp.float32)
    away = lax.dynamic_slice_in_dim(total, (1 - low) * 128, 128, axis=0)
    keep = lax.dynamic_slice_in_dim(total, low * 128, 128, axis=0)
    return (keep + swap_low(away.astype(jnp.bfloat16)).astype(jnp.float32))[None]


def after(values, *others):
    return lax.optimization_barrier((values, others))[0]


CAPACITY = 24
NOTES = 128


def exchange(value):
    devices = lax.axis_size("expert")
    blocks = value.reshape(devices, CAPACITY, value.shape[1])
    blocks = lax.all_to_all(blocks, "expert", split_axis=0, concat_axis=0, tiled=True)
    return blocks.reshape(value.shape)


def local(tokens, cotangent, prob, assign, w_gate, w_up, w_down):
    gate_weight, up_weight, down_weight = w_gate[0], w_up[0], w_down[0]
    count, width = tokens.shape
    slots = lax.axis_size("expert") * CAPACITY
    index = lax.axis_index("dp")
    low = index % 2
    position = (index // 2).astype(jnp.int32).reshape(1)
    size = gate_weight.shape[1]
    weight = prob.astype(jnp.float32).reshape(1, count)
    work = 2 * slots * width * size
    both, slot = call(
        send_kernel,
        (
            jax.ShapeDtypeStruct((slots, 2 * width), jnp.bfloat16),
            jax.ShapeDtypeStruct((1, count), jnp.int32),
        ),
        position,
        (assign.reshape(1, count), weight, tokens, cotangent),
        work // 2,
    )
    both = exchange(both)
    leaving, far_low, far_high, ready_up, ready_down, add_up, add_down, own = expert(
        position, both, gate_weight, up_weight, down_weight
    )
    home = exchange(leaving)
    got = lax.optimization_barrier(first_step(far_low, far_high))
    ready = (shift_y(ready_up, 1), shift_y(ready_down, -1))
    cuts = [slice(n * BLOCK, n * BLOCK + BLOCK) for n in range(3)]
    second, values = [], ()
    for cut in cuts:
        values = second_values(
            *after((add_up[cut], add_down[cut]), values), [value[cut] for value in got]
        )
        second.append((shift_y(values[0], 1), shift_y(values[1], -1)))
    parts = []
    for place, (cut, added) in enumerate(zip(cuts, second)):
        mine = after(own[cut], parts[0]) if place == 2 else own[cut]
        parts.append(third_step(mine, [value[cut] for value in ready], added, low))
    grad_tokens, grad_prob = call(
        home_kernel,
        (
            jax.ShapeDtypeStruct((count, width), jnp.bfloat16),
            jax.ShapeDtypeStruct((1, count), jnp.float32),
        ),
        position,
        (slot, weight, home),
        2 * count * slots * width,
    )
    grad_prob = grad_prob.reshape(count).astype(jnp.bfloat16)
    return (grad_tokens, grad_prob, parts[1], parts[2], parts[0])


def solution(mesh):
    placed = (
        P(("dp", "expert"), None),
        P(("dp", "expert"), None),
        P(("dp", "expert")),
        P(("dp", "expert"), None),
        P("expert", None, None),
        P("expert", None, None),
        P("expert", None, None),
    )
    return jax.shard_map(
        local,
        mesh=mesh,
        in_specs=placed,
        out_specs=(
            P(("dp", "expert"), None),
            P(("dp", "expert")),
            P("expert", "dp", None),
            P("expert", "dp", None),
            P("expert", "dp", None),
        ),
        check_vma=False,
    )
```

```python
import jax
import jax.numpy as jnp
from jax import lax
from jax.experimental import pallas as pl
from jax.experimental.pallas import tpu as pltpu
from jax.sharding import PartitionSpec as P


def shift_y(value, step):
    pairs = []
    for dp in range(8):
        y, low = divmod(dp, 2)
        pairs.append((dp, ((y + step) % 4) * 2 + low))
    return lax.ppermute(value, "dp", pairs)


def swap_low(value):
    return lax.ppermute(value, "dp", [(dp, dp ^ 1) for dp in range(8)])


HALF = 512
BLOCK = 256
LEFT_TURNED = (((0,), (0,)), ((), ()))
RIGHT_TURNED = (((1,), (1,)), ((), ()))


def product(left, right, dimensions):
    return lax.dot_general(left, right, dimensions, preferred_element_type=jnp.float32)


def call(kernel, outputs, position, inputs, flops):
    in_vmem = pl.BlockSpec(memory_space=pltpu.VMEM)
    in_smem = pl.BlockSpec(memory_space=pltpu.SMEM)
    moved = sum(v.size * v.dtype.itemsize for v in inputs)
    return pl.pallas_call(
        kernel,
        out_shape=outputs,
        in_specs=[in_smem] + [in_vmem] * len(inputs),
        out_specs=[in_vmem] * len(outputs),
        compiler_params=pltpu.CompilerParams(vmem_limit_bytes=16 * 1024 * 1024),
        cost_estimate=pl.CostEstimate(flops=flops, bytes_accessed=moved, transcendentals=0),
    )(position, *inputs)


def columns_of(ref, y, offset):
    start = pl.multiple_of(((y + offset) % 4) * BLOCK, BLOCK)
    return ref[:, pl.ds(start, BLOCK)]


def expert_kernel(
    position,
    both,
    w_gate,
    w_up,
    w_down,
    leaving,
    far_low,
    far_high,
    ready_up,
    ready_down,
    add_up,
    add_down,
    own,
    hidden,
    gate_pre,
    up_pre,
):
    y = position[0]
    width = w_gate.shape[0]
    moved = jnp.zeros((both.shape[0], 1), jnp.float32)
    for start in range(0, w_gate.shape[1], BLOCK):
        cut = pl.ds(start, BLOCK)
        gate = jnp.dot(both[:, :width], w_gate[:, cut], preferred_element_type=jnp.float32)
        up = jnp.dot(both[:, :width], w_up[:, cut], preferred_element_type=jnp.float32)
        grad_hidden = product(both[:, width:], w_down[cut, :], RIGHT_TURNED)
        sigmoid_gate = jax.nn.sigmoid(gate)
        active = gate * sigmoid_gate
        held = (active * up).astype(jnp.bfloat16)
        hidden[:, cut] = held
        slope = sigmoid_gate * (1.0 + gate * (1.0 - sigmoid_gate))
        gate_pre[:, cut] = (grad_hidden * up * slope).astype(jnp.bfloat16)
        up_pre[:, cut] = (grad_hidden * active).astype(jnp.bfloat16)
        part = held.astype(jnp.float32) * grad_hidden
        moved = moved + jnp.sum(part, axis=1, keepdims=True)

    scaled = both.at[:, width:]
    pairs = ((hidden, scaled), (both, gate_pre), (both, up_pre))
    cuts = [pl.ds(place * BLOCK, BLOCK) for place in range(3)]
    for cut, (left, right) in zip(cuts, pairs):
        far = product(columns_of(left, y, 2), right[...], LEFT_TURNED).astype(jnp.bfloat16)
        far_low[cut, :] = far[:, :HALF]
        far_high[cut, :] = far[:, HALF:]
    leaving[:, width:] = jnp.broadcast_to(moved, (both.shape[0], NOTES)).astype(jnp.bfloat16)
    for start in range(0, width, BLOCK):
        cut = pl.ds(start, BLOCK)
        grad = product(gate_pre[...], w_gate[cut, :], RIGHT_TURNED)
        grad = grad + product(up_pre[...], w_up[cut, :], RIGHT_TURNED)
        leaving[:, cut] = grad.astype(jnp.bfloat16)
    for cut, (left, right) in zip(cuts, pairs):
        part = product(columns_of(left, y, 0), right[...], LEFT_TURNED)
        own[cut, :] = part.astype(jnp.bfloat16)
    for cut, (left, right) in zip(cuts, pairs):
        part = product(columns_of(left, y, 1), right[...], LEFT_TURNED)
        add_up[cut, :] = part[:, :HALF].astype(jnp.bfloat16)
        ready_up[cut, :] = part[:, HALF:].astype(jnp.bfloat16)
        part = product(columns_of(left, y, 3), right[...], LEFT_TURNED)
        add_down[cut, :] = part[:, HALF:].astype(jnp.bfloat16)
        ready_down[cut, :] = part[:, :HALF].astype(jnp.bfloat16)


def expert(position, both, w_gate, w_up, w_down):
    slots, width = both.shape[0], w_gate.shape[0]
    size = w_gate.shape[1]
    shapes = [((slots, width + NOTES), jnp.bfloat16)]
    shapes += [((3 * BLOCK, HALF), jnp.bfloat16)] * 6
    shapes += [((3 * BLOCK, width), jnp.bfloat16)]
    in_vmem = pl.BlockSpec(memory_space=pltpu.VMEM)
    return pl.pallas_call(
        expert_kernel,
        out_shape=[jax.ShapeDtypeStruct(*shape) for shape in shapes],
        in_specs=[pl.BlockSpec(memory_space=pltpu.SMEM)] + [in_vmem] * 4,
        out_specs=[in_vmem] * len(shapes),
        scratch_shapes=[pltpu.VMEM((slots, size), jnp.bfloat16)] * 3,
        compiler_params=pltpu.CompilerParams(vmem_limit_bytes=24 * 1024 * 1024),
        cost_estimate=pl.CostEstimate(
            flops=16 * slots * width * size, bytes_accessed=20_000_000, transcendentals=0
        ),
    )(position, both, w_gate, w_up, w_down)


def pick_of(slot, slots):
    return (lax.broadcasted_iota(jnp.int32, (slots, slot.shape[1]), 0) == slot).astype(
        jnp.bfloat16
    )


def send_kernel(position, named, prob, tokens, cotangent, both, slot):
    count, width = tokens.shape
    square = (count, count)
    across = jnp.broadcast_to(named[...], square)
    earlier = lax.broadcasted_iota(jnp.int32, square, 0) < lax.broadcasted_iota(
        jnp.int32, square, 1
    )
    same = jnp.where(earlier & (across.T == across), 1, 0)
    slot[...] = named[...] * CAPACITY + jnp.sum(same, axis=0, keepdims=True)
    pick = pick_of(slot[...], both.shape[0])
    both[:, :width] = jnp.dot(pick, tokens[...], preferred_element_type=jnp.float32).astype(
        jnp.bfloat16
    )
    weight = jnp.broadcast_to(prob[...], square).T[:, :1]
    scaled = (weight * cotangent[...].astype(jnp.float32)).astype(jnp.bfloat16)
    both[:, width:] = jnp.dot(pick, scaled, preferred_element_type=jnp.float32).astype(
        jnp.bfloat16
    )


def home_kernel(position, slot, prob, home, grad_tokens, grad_prob):
    width = grad_tokens.shape[1]
    pick = pick_of(slot[...], home.shape[0])
    grad_tokens[...] = product(pick, home[:, :width], LEFT_TURNED).astype(jnp.bfloat16)
    moved = product(home[:, width:], pick, LEFT_TURNED)
    grad_prob[...] = moved[:1, :] / prob[...]


def first_step(low, high):
    return shift_y(low, 1), shift_y(high, -1)


def second_values(up_part, down_part, got):
    up_part = (up_part.astype(jnp.float32) + got[0].astype(jnp.float32)).astype(jnp.bfloat16)
    down_part = (down_part.astype(jnp.float32) + got[1].astype(jnp.float32)).astype(jnp.bfloat16)
    return lax.optimization_barrier((up_part, down_part))


def third_step(own, ready, added, low):
    left = jnp.concatenate([added[0], ready[0]], axis=1)
    right = jnp.concatenate([ready[1], added[1]], axis=1)
    total = own.astype(jnp.float32) + left.astype(jnp.float32) + right.astype(jnp.float32)
    away = lax.dynamic_slice_in_dim(total, (1 - low) * 128, 128, axis=0)
    keep = lax.dynamic_slice_in_dim(total, low * 128, 128, axis=0)
    return (keep + swap_low(away.astype(jnp.bfloat16)).astype(jnp.float32))[None]


def after(values, *others):
    return lax.optimization_barrier((values, others))[0]


CAPACITY = 24
NOTES = 128


def exchange(value):
    devices = lax.axis_size("expert")
    blocks = value.reshape(devices, CAPACITY, value.shape[1])
    blocks = lax.all_to_all(blocks, "expert", split_axis=0, concat_axis=0, tiled=True)
    return blocks.reshape(value.shape)


def local(tokens, cotangent, prob, assign, w_gate, w_up, w_down):
    gate_weight, up_weight, down_weight = w_gate[0], w_up[0], w_down[0]
    count, width = tokens.shape
    slots = lax.axis_size("expert") * CAPACITY
    index = lax.axis_index("dp")
    low = index % 2
    position = (index // 2).astype(jnp.int32).reshape(1)
    size = gate_weight.shape[1]
    weight = prob.astype(jnp.float32).reshape(1, count)
    work = 2 * slots * width * size
    both, slot = call(
        send_kernel,
        (
            jax.ShapeDtypeStruct((slots, 2 * width), jnp.bfloat16),
            jax.ShapeDtypeStruct((1, count), jnp.int32),
        ),
        position,
        (assign.reshape(1, count), weight, tokens, cotangent),
        work // 2,
    )
    both = exchange(both)
    leaving, far_low, far_high, ready_up, ready_down, add_up, add_down, own = expert(
        position, both, gate_weight, up_weight, down_weight
    )
    home = exchange(leaving)
    got = lax.optimization_barrier(first_step(far_low, far_high))
    ready = (shift_y(ready_up, 1), shift_y(ready_down, -1))
    cuts = [slice(n * BLOCK, n * BLOCK + BLOCK) for n in range(3)]
    second, values = [], ()
    for cut in cuts:
        values = second_values(
            *after((add_up[cut], add_down[cut]), values), [value[cut] for value in got]
        )
        second.append((shift_y(values[0], 1), shift_y(values[1], -1)))
    grad_tokens, grad_prob = call(
        home_kernel,
        (
            jax.ShapeDtypeStruct((count, width), jnp.bfloat16),
            jax.ShapeDtypeStruct((1, count), jnp.float32),
        ),
        position,
        (slot, weight, home),
        2 * count * slots * width,
    )
    parts = []
    for place, (cut, added) in enumerate(zip(cuts, second)):
        ahead = (*parts, grad_tokens) if place == 2 else values
        mine = after(own[cut], ahead)
        parts.append(third_step(mine, [value[cut] for value in ready], added, low))
    grad_prob = grad_prob.reshape(count).astype(jnp.bfloat16)
    return (grad_tokens, grad_prob, parts[1], parts[2], parts[0])


def solution(mesh):
    placed = (
        P(("dp", "expert"), None),
        P(("dp", "expert"), None),
        P(("dp", "expert")),
        P(("dp", "expert"), None),
        P("expert", None, None),
        P("expert", None, None),
        P("expert", None, None),
    )
    return jax.shard_map(
        local,
        mesh=mesh,
        in_specs=placed,
        out_specs=(
            P(("dp", "expert"), None),
            P(("dp", "expert")),
            P("expert", "dp", None),
            P("expert", "dp", None),
            P("expert", "dp", None),
        ),
        check_vma=False,
    )
```

```python
import jax
import jax.numpy as jnp
from jax import lax
from jax.experimental import pallas as pl
from jax.experimental.pallas import tpu as pltpu
from jax.sharding import PartitionSpec as P


def shift_y(value, step):
    pairs = []
    for dp in range(8):
        y, low = divmod(dp, 2)
        pairs.append((dp, ((y + step) % 4) * 2 + low))
    return lax.ppermute(value, "dp", pairs)


def swap_low(value):
    return lax.ppermute(value, "dp", [(dp, dp ^ 1) for dp in range(8)])


HALF = 512
BLOCK = 256
LEFT_TURNED = (((0,), (0,)), ((), ()))
RIGHT_TURNED = (((1,), (1,)), ((), ()))


def product(left, right, dimensions):
    return lax.dot_general(left, right, dimensions, preferred_element_type=jnp.float32)


def call(kernel, outputs, position, inputs, flops):
    in_vmem = pl.BlockSpec(memory_space=pltpu.VMEM)
    in_smem = pl.BlockSpec(memory_space=pltpu.SMEM)
    moved = sum(v.size * v.dtype.itemsize for v in inputs)
    return pl.pallas_call(
        kernel,
        out_shape=outputs,
        in_specs=[in_smem] + [in_vmem] * len(inputs),
        out_specs=[in_vmem] * len(outputs),
        compiler_params=pltpu.CompilerParams(vmem_limit_bytes=16 * 1024 * 1024),
        cost_estimate=pl.CostEstimate(flops=flops, bytes_accessed=moved, transcendentals=0),
    )(position, *inputs)


def columns_of(ref, y, offset):
    start = pl.multiple_of(((y + offset) % 4) * BLOCK, BLOCK)
    return ref[:, pl.ds(start, BLOCK)]


def expert_kernel(
    position,
    both,
    w_gate,
    w_up,
    w_down,
    leaving,
    far_low,
    far_high,
    ready_up,
    ready_down,
    add_up,
    add_down,
    own,
    hidden,
    gate_pre,
    up_pre,
):
    y = position[0]
    width = w_gate.shape[0]
    moved = jnp.zeros((both.shape[0], 1), jnp.float32)
    for start in range(0, w_gate.shape[1], BLOCK):
        cut = pl.ds(start, BLOCK)
        gate = jnp.dot(both[:, :width], w_gate[:, cut], preferred_element_type=jnp.float32)
        up = jnp.dot(both[:, :width], w_up[:, cut], preferred_element_type=jnp.float32)
        grad_hidden = product(both[:, width:], w_down[cut, :], RIGHT_TURNED)
        sigmoid_gate = jax.nn.sigmoid(gate)
        active = gate * sigmoid_gate
        held = (active * up).astype(jnp.bfloat16)
        hidden[:, cut] = held
        slope = sigmoid_gate * (1.0 + gate * (1.0 - sigmoid_gate))
        gate_pre[:, cut] = (grad_hidden * up * slope).astype(jnp.bfloat16)
        up_pre[:, cut] = (grad_hidden * active).astype(jnp.bfloat16)
        part = held.astype(jnp.float32) * grad_hidden
        moved = moved + jnp.sum(part, axis=1, keepdims=True)

    scaled = both.at[:, width:]
    pairs = ((hidden, scaled), (both, gate_pre), (both, up_pre))
    cuts = [pl.ds(place * BLOCK, BLOCK) for place in range(3)]
    for cut, (left, right) in zip(cuts, pairs):
        far = product(columns_of(left, y, 2), right[...], LEFT_TURNED).astype(jnp.bfloat16)
        far_low[cut, :] = far[:, :HALF]
        far_high[cut, :] = far[:, HALF:]
    leaving[:, width:] = jnp.broadcast_to(moved, (both.shape[0], NOTES)).astype(jnp.bfloat16)
    for start in range(0, width, BLOCK):
        cut = pl.ds(start, BLOCK)
        grad = product(gate_pre[...], w_gate[cut, :], RIGHT_TURNED)
        grad = grad + product(up_pre[...], w_up[cut, :], RIGHT_TURNED)
        leaving[:, cut] = grad.astype(jnp.bfloat16)
    for cut, (left, right) in zip(cuts, pairs):
        part = product(columns_of(left, y, 0), right[...], LEFT_TURNED)
        own[cut, :] = part.astype(jnp.bfloat16)
    for cut, (left, right) in zip(cuts, pairs):
        part = product(columns_of(left, y, 1), right[...], LEFT_TURNED)
        add_up[cut, :] = part[:, :HALF].astype(jnp.bfloat16)
        ready_up[cut, :] = part[:, HALF:].astype(jnp.bfloat16)
        part = product(columns_of(left, y, 3), right[...], LEFT_TURNED)
        add_down[cut, :] = part[:, HALF:].astype(jnp.bfloat16)
        ready_down[cut, :] = part[:, :HALF].astype(jnp.bfloat16)


def expert(position, both, w_gate, w_up, w_down):
    slots, width = both.shape[0], w_gate.shape[0]
    size = w_gate.shape[1]
    shapes = [((slots, width + NOTES), jnp.bfloat16)]
    shapes += [((3 * BLOCK, HALF), jnp.bfloat16)] * 6
    shapes += [((3 * BLOCK, width), jnp.bfloat16)]
    in_vmem = pl.BlockSpec(memory_space=pltpu.VMEM)
    return pl.pallas_call(
        expert_kernel,
        out_shape=[jax.ShapeDtypeStruct(*shape) for shape in shapes],
        in_specs=[pl.BlockSpec(memory_space=pltpu.SMEM)] + [in_vmem] * 4,
        out_specs=[in_vmem] * len(shapes),
        scratch_shapes=[pltpu.VMEM((slots, size), jnp.bfloat16)] * 3,
        compiler_params=pltpu.CompilerParams(vmem_limit_bytes=24 * 1024 * 1024),
        cost_estimate=pl.CostEstimate(
            flops=16 * slots * width * size, bytes_accessed=20_000_000, transcendentals=0
        ),
    )(position, both, w_gate, w_up, w_down)


def pick_of(slot, slots):
    return (lax.broadcasted_iota(jnp.int32, (slots, slot.shape[1]), 0) == slot).astype(
        jnp.bfloat16
    )


def send_kernel(position, named, prob, tokens, cotangent, both, slot):
    count, width = tokens.shape
    square = (count, count)
    across = jnp.broadcast_to(named[...], square)
    earlier = lax.broadcasted_iota(jnp.int32, square, 0) < lax.broadcasted_iota(
        jnp.int32, square, 1
    )
    same = jnp.where(earlier & (across.T == across), 1, 0)
    slot[...] = named[...] * CAPACITY + jnp.sum(same, axis=0, keepdims=True)
    pick = pick_of(slot[...], both.shape[0])
    both[:, :width] = jnp.dot(pick, tokens[...], preferred_element_type=jnp.float32).astype(
        jnp.bfloat16
    )
    weight = jnp.broadcast_to(prob[...], square).T[:, :1]
    scaled = (weight * cotangent[...].astype(jnp.float32)).astype(jnp.bfloat16)
    both[:, width:] = jnp.dot(pick, scaled, preferred_element_type=jnp.float32).astype(
        jnp.bfloat16
    )


def home_kernel(position, slot, prob, home, grad_tokens, grad_prob):
    width = grad_tokens.shape[1]
    pick = pick_of(slot[...], home.shape[0])
    grad_tokens[...] = product(pick, home[:, :width], LEFT_TURNED).astype(jnp.bfloat16)
    moved = product(home[:, width:], pick, LEFT_TURNED)
    grad_prob[...] = moved[:1, :] / prob[...]


def first_step(low, high):
    return shift_y(low, 1), shift_y(high, -1)


def second_values(up_part, down_part, got):
    up_part = (up_part.astype(jnp.float32) + got[0].astype(jnp.float32)).astype(jnp.bfloat16)
    down_part = (down_part.astype(jnp.float32) + got[1].astype(jnp.float32)).astype(jnp.bfloat16)
    return lax.optimization_barrier((up_part, down_part))


def third_step(own, ready, added, low):
    left = jnp.concatenate([added[0], ready[0]], axis=1)
    right = jnp.concatenate([ready[1], added[1]], axis=1)
    total = own.astype(jnp.float32) + left.astype(jnp.float32) + right.astype(jnp.float32)
    away = lax.dynamic_slice_in_dim(total, (1 - low) * 128, 128, axis=0)
    keep = lax.dynamic_slice_in_dim(total, low * 128, 128, axis=0)
    return (keep + swap_low(away.astype(jnp.bfloat16)).astype(jnp.float32))[None]


def after(values, *others):
    return lax.optimization_barrier((values, others))[0]


CAPACITY = 24
NOTES = 128


def exchange(value):
    devices = lax.axis_size("expert")
    blocks = value.reshape(devices, CAPACITY, value.shape[1])
    blocks = lax.all_to_all(blocks, "expert", split_axis=0, concat_axis=0, tiled=True)
    return blocks.reshape(value.shape)


def local(tokens, cotangent, prob, assign, w_gate, w_up, w_down):
    gate_weight, up_weight, down_weight = w_gate[0], w_up[0], w_down[0]
    count, width = tokens.shape
    slots = lax.axis_size("expert") * CAPACITY
    index = lax.axis_index("dp")
    low = index % 2
    position = (index // 2).astype(jnp.int32).reshape(1)
    size = gate_weight.shape[1]
    weight = prob.astype(jnp.float32).reshape(1, count)
    work = 2 * slots * width * size
    both, slot = call(
        send_kernel,
        (
            jax.ShapeDtypeStruct((slots, 2 * width), jnp.bfloat16),
            jax.ShapeDtypeStruct((1, count), jnp.int32),
        ),
        position,
        (assign.reshape(1, count), weight, tokens, cotangent),
        work // 2,
    )
    both = exchange(both)
    leaving, far_low, far_high, ready_up, ready_down, add_up, add_down, own = expert(
        position, both, gate_weight, up_weight, down_weight
    )
    home = exchange(leaving)
    got = lax.optimization_barrier(first_step(far_low, far_high))
    ready = (shift_y(ready_up, 1), shift_y(ready_down, -1))
    cuts = [slice(n * BLOCK, n * BLOCK + BLOCK) for n in range(3)]
    second, values = [], ()
    for cut in cuts:
        values = second_values(
            *after((add_up[cut], add_down[cut]), values), [value[cut] for value in got]
        )
        second.append((shift_y(values[0], 1), shift_y(values[1], -1)))
    parts = []
    for place, (cut, added) in enumerate(zip(cuts, second)):
        mine = after(own[cut], parts[0]) if place == 2 else after(own[cut], values)
        parts.append(third_step(mine, [value[cut] for value in ready], added, low))
    grad_tokens, grad_prob = call(
        home_kernel,
        (
            jax.ShapeDtypeStruct((count, width), jnp.bfloat16),
            jax.ShapeDtypeStruct((1, count), jnp.float32),
        ),
        position,
        (slot, weight, home),
        2 * count * slots * width,
    )
    grad_prob = grad_prob.reshape(count).astype(jnp.bfloat16)
    return (grad_tokens, grad_prob, parts[1], parts[2], parts[0])


def solution(mesh):
    placed = (
        P(("dp", "expert"), None),
        P(("dp", "expert"), None),
        P(("dp", "expert")),
        P(("dp", "expert"), None),
        P("expert", None, None),
        P("expert", None, None),
        P("expert", None, None),
    )
    return jax.shard_map(
        local,
        mesh=mesh,
        in_specs=placed,
        out_specs=(
            P(("dp", "expert"), None),
            P(("dp", "expert")),
            P("expert", "dp", None),
            P("expert", "dp", None),
            P("expert", "dp", None),
        ),
        check_vma=False,
    )
```
